512 devices in a mesh: mem: 16 (over x_lo, y, core), tile: 32 (over x_hi, z).
Axes of the slice: x: 4 (x_hi: 2, x_lo: 2; x = x_hi * 2 + x_lo), y: 4, z: 16, core: 2. Of those that a mesh axis runs over, the one named last changes fastest.
Arguments:
- perturbations: bfloat16 [32, 16, 512, 512], P('mem', None, 'tile'), may hold values from -6 to 6
- control: float32 [32, 16, 512, 512], P('mem', None, 'tile'), may hold values from -6 to 6
- innovation: float32 [16, 512, 512], P(None, 'tile'), may hold values from -6 to 6
- precision_field: float32 [16, 512, 512], P(None, 'tile'), may hold values from 0.2 to 5
- smooth_kernel: float32 [5, 5], replicated, may hold values from 0.2 to 1
- vertical_loc: float32 [16, 16], replicated, may hold values from -1.5 to 1.5
Outputs:
- increment: float32 [16, 512, 512], P(None, 'tile')
- gradient: float32 [32, 16, 512, 512], P('mem', None, 'tile')
The draws below stay inside these ranges and needn't reach their ends.
All inputs are finite; a program needn't handle non-finite values.
Results may differ from the reference program's by a relative error of at most 0.0003.
Values sent between devices are 32-bit elements; how exact they have to be, the bound alone decides.
A program may use at most 64 MiB of HBM per device.

```python
import math
import jax
import jax.numpy as jnp
from jax import lax

LEV = 16
LAT = 512
MEMBERS = 32
NLON = 512


def shard_levels(rng, extent, pieces, low, top_value):
    gain = 1.0
    for dim, parts in pieces:
        heights = jax.random.uniform(jax.random.fold_in(jax.random.fold_in(rng, 6), dim), (parts,), jnp.float32, low / len(pieces), top_value / len(pieces))
        gain = gain * jnp.repeat(jnp.exp(heights), extent[dim] // parts).reshape((-1,) + (1,) * (len(extent) - 1 - dim))
    return gain


def centred(key, dims, deviation, most, pieces=(), dtype=jnp.bfloat16):
    gain = shard_levels(key, dims, pieces, -0.22, 0.18) if pieces else 1.0
    values = jax.random.normal(key, dims, jnp.float32) * deviation * gain
    return jnp.minimum(jnp.maximum(values, -most), most).astype(dtype)


def setup_inputs(seed: int = 0) -> dict:
    arg_keys = jax.random.split(jax.random.key(seed), 7)
    perturbations = centred(arg_keys[0], (MEMBERS, LEV, NLON, LAT), 1.0, 6.0, ((0, 16), (2, 32)))
    control = centred(arg_keys[1], (MEMBERS, LEV, NLON, LAT), 1.0, 6.0, ((0, 16), (2, 32)), jnp.float32)
    innovation = centred(arg_keys[2], (LEV, NLON, LAT), 1.0, 6.0, ((1, 32),), jnp.float32)
    precision_field = jnp.clip(jnp.exp(math.log(5.0) - 3.218876 * jax.random.uniform(arg_keys[3], (LEV, NLON, LAT), jnp.float32) ** shard_levels(arg_keys[3], (LEV, NLON, LAT), ((1, 32),), -0.2, 0.2)), 0.2, 5.0)
    smooth_kernel = jnp.clip(jax.random.uniform(arg_keys[4], (5, 5), jnp.float32, 0.2, 1.0), 0.2, 1.0)
    vertical_loc = centred(arg_keys[5], (LEV, LEV), LEV ** -0.5, 1.5, (), jnp.float32)
    return dict(perturbations=perturbations, control=control, innovation=innovation, precision_field=precision_field, smooth_kernel=smooth_kernel, vertical_loc=vertical_loc)


def smooth_pass(field, weights):
    lon_ext = jnp.concatenate([field[..., -2:, :], field, field[..., :2, :]], axis=-2)
    zeros_pad = jnp.zeros(lon_ext.shape[:-1] + (2,), jnp.float32)
    padded = jnp.concatenate([zeros_pad, lon_ext, zeros_pad], axis=-1)
    width = field.shape[-2]
    rows = field.shape[-1]
    total = jnp.zeros(field.shape, jnp.float32)
    for a in range(5):
        for b in range(5):
            total = total + weights[a, b] * padded[..., a:a + width, b:b + rows]
    return total

def localize(member_control, weights, vertical_loc):
    mixed = jnp.einsum('lm,mij->lij', vertical_loc, member_control, precision=lax.Precision.HIGHEST)
    for step in range(4):
        mixed = smooth_pass(mixed, weights)
    return mixed

def reference(perturbations, control, innovation, precision_field, smooth_kernel, vertical_loc):
    weights = smooth_kernel / jnp.sum(smooth_kernel)

    def accumulate(total, pair):
        member_pert, member_control = pair
        local = localize(member_control, weights, vertical_loc)
        return (total + member_pert.astype(jnp.float32) * local, None)
    start = jnp.zeros(innovation.shape, jnp.float32)
    increment, unused = lax.scan(accumulate, start, (perturbations, control))
    weighted = precision_field * (increment - innovation)

    def member_gradient(pair):
        member_pert, member_control = pair
        outputs, pullback = jax.vjp(lambda c: localize(c, weights, vertical_loc), member_control)
        back = pullback(member_pert.astype(jnp.float32) * weighted)[0]
        return member_control + back
    gradient = lax.map(member_gradient, (perturbations, control))
    return (increment, gradient)
```

```python
import functools

import jax
import jax.numpy as jnp
from jax import lax
from jax.experimental import pallas as pl
from jax.experimental.pallas import tpu as pltpu
from jax.sharding import PartitionSpec as P

MESH = pl.DeviceIdType.MESH
HIGHEST = lax.Precision.HIGHEST
F32 = jnp.float32
BF16 = jnp.bfloat16


def lanes_of(shape):
    return lax.broadcasted_iota(jnp.int32, shape, len(shape) - 1)


def rows_of(shape):
    return lax.broadcasted_iota(jnp.int32, shape, len(shape) - 2)


def roll(x, shift):
    return pltpu.roll(x, shift % x.shape[-1], x.ndim - 1)


def composed_rows(sk, flip, variant):
    shape = (16, 1024)
    lane = lanes_of(shape)
    col = lane % 32
    start = jnp.where(lane == 264 + rows_of(shape), 1.0, 0.0).astype(F32)
    if variant == 0:
        inside = col >= 8
    elif variant == 2:
        inside = col < 24
    else:
        inside = None

    def tap(a, b):
        return sk[4 - a, 4 - b] if flip else sk[a, b]

    def one_pass(step, r):
        moved = [roll(r, 32 * (a - 2)) if a != 2 else r for a in range(5)]
        out = None
        for b in range(5):
            part = moved[0] * tap(0, b)
            for a in range(1, 5):
                part = part + moved[a] * tap(a, b)
            part = roll(part, b - 2) if b != 2 else part
            out = part if out is None else out + part
        if inside is not None:
            out = jnp.where(inside, out, 0.0)
        return out

    r = lax.fori_loop(0, 4, one_pass, start)
    total = sk[0, 0]
    for n in range(1, 25):
        total = total + sk[n // 5, n % 5]
    total = jnp.full((16, 1024), total, F32)
    square = total * total
    return r / (square * square)


def split(x):
    hi = x.astype(BF16)
    lo = (x - hi.astype(F32)).astype(BF16)
    return hi, lo


def kernel(
    ctl_h, pert_h, innov_h, prec_h, sk, vloc,
    inc_h, grad_h,
    ctl_v, pert_v, pert_f, innov_v, prec_v, xc, pt, xb, w_own, w_left, w_right, field,
    contrib, core_in, chip_sum, parts_in, inc_all, halo_w, own_w, prec_p, innov_p, grad_v, inc_v,
    in_sem, out_sem, c_send, c_recv, p_send, p_recv, k_send, k_recv, r_send, r_recv,
    a_send, a_recv, h_send, h_recv, f_send, f_recv, g_send, g_recv,
):
    m = lax.axis_index("mem")
    t = lax.axis_index("tile")
    tiles = lax.axis_size("tile")
    right = lax.rem(t + 1, tiles)
    left = lax.rem(t + tiles - 1, tiles)
    chip = m // 2
    core = m % 2
    sibling = 2 * chip + 1 - core

    loads = [
        [
            pltpu.make_async_copy(src.at[:, pl.ds(128 * q, 128)], dst.at[q], in_sem.at[n, q])
            for q in range(4)
        ]
        for n, (src, dst) in enumerate(
            [(ctl_h, ctl_v), (pert_h, pert_v), (innov_h, innov_v), (prec_h, prec_v)]
        )
    ]
    for load in loads:
        for copy in load:
            copy.start()

    def arrive(n):
        for copy in loads[n]:
            copy.wait()

    def peer(d):
        other = jnp.bitwise_xor(chip, d)
        return other, 2 * other + core

    barrier = pltpu.get_barrier_semaphore()

    def greet(mem, tile):
        pl.semaphore_signal(barrier, inc=1, device_id=(mem, tile), device_id_type=MESH)

    greet(sibling, t)
    for d in range(1, 8):
        greet(peer(d)[1], t)
    for k in range(4):
        greet(2 * k + core, right)
        greet(2 * (k + 4) + core, left)
    greet(m, jnp.where(chip < 4, left, right))

    col16 = lanes_of((128, 16))
    row128 = rows_of((128, 16))
    pick = jnp.where(row128 % 16 == col16, 1.0, 0.0).astype(F32)
    wide = jnp.dot(pick, vloc[...], precision=HIGHEST, preferred_element_type=F32)
    lane16 = lanes_of((16, 128))
    spread = jnp.where(lane16 % 16 == rows_of((16, 128)), 1.0, 0.0).astype(F32)
    full = jnp.dot(wide, spread, precision=HIGHEST, preferred_element_type=F32)
    same = rows_of((128, 128)) // 16 == lanes_of((128, 128)) // 16
    mix = jnp.where(same, full, 0.0)
    mix_t = mix.T

    def columns(ref, i, count):
        return [ref[q, pl.ds(i, count, stride=16), :] for q in range(4)]

    def remote(src, dst, send, recv, mem, tile):
        return pltpu.make_async_remote_copy(
            src_ref=src, dst_ref=dst, send_sem=send, recv_sem=recv,
            device_id=(mem, tile), device_id_type=MESH,
        )

    arrive(0)
    c_copies = []
    for n, group in enumerate([range(8, 12), range(0, 4), range(12, 16), range(4, 8)]):
        for i in group:
            x = jnp.concatenate(columns(ctl_v, i, 32), axis=0)
            x = jnp.dot(mix, x, precision=HIGHEST, preferred_element_type=F32)
            xc[8 + i] = x.T
        if n == 0:
            pl.semaphore_wait(barrier, 17)
        first = group[0]
        to_right = first >= 8
        target = first - 8 if to_right else 24 + first
        copy = remote(
            xc.at[pl.ds(8 + first, 4)], xc.at[pl.ds(target, 4)],
            c_send.at[n], c_recv.at[n], m, right if to_right else left,
        )
        copy.start()
        c_copies.append(copy)

    lane8 = lanes_of((8, 128))

    def prepare(index, x):
        top = jnp.where(lane8 >= 32, roll(x[120:128], 32), 0.0)
        bottom = jnp.where(lane8 < 96, roll(x[0:8], -32), 0.0)
        hi, lo = split(jnp.concatenate([top, x, bottom], axis=0))
        xb[index, :, 0:128] = hi
        xb[index, :, 128:256] = lo

    def each(first, last, body):
        def step(i, carry):
            body(i)
            return carry

        lax.fori_loop(first, last, step, 0)

    each(8, 24, lambda i: prepare(i, xc[i]))

    def build(direction):
        for variant in range(3):
            base = composed_rows(sk, direction == 1, variant)
            for i in range(16):
                hi, lo = split(roll(base, 32 * i) if i else base)
                at = 16 * i
                w_own[direction, variant, at : at + 16, :] = hi[:, 256:768]
                w_own[direction, variant, 256 + at : 272 + at, :] = lo[:, 256:768]
                if i < 8:
                    w_left[direction, variant, at : at + 16, :] = hi[:, 0:256]
                    w_left[direction, variant, 128 + at : 144 + at, :] = lo[:, 0:256]
                else:
                    w_right[direction, variant, at - 128 : at - 112, :] = hi[:, 768:1024]
                    w_right[direction, variant, at : at + 16, :] = lo[:, 768:1024]

    build(0)

    lane3 = lanes_of((1, 1, 128))

    def block(w, lons, rows):
        first, last = lons
        rhs = xb[first:last, rows, :].reshape((last - first) * 32, 256)
        out = jnp.dot(w[...], rhs, preferred_element_type=F32)
        half = out.shape[0] // 2
        out = out[:half, :128] + out[:half, 128:] + out[half:, :128]
        return out.reshape(half // 16, 16, 128)

    def smooth(weights, direction, lons, put):
        def at(variant, b):
            rows = pl.ds(pl.multiple_of(16 * b, 16), 32)
            return block(weights.at[direction, variant], lons, rows)

        each(1, 7, lambda b: put(pl.ds(pl.multiple_of(16 * b, 16), 16), at(1, b)))
        put(pl.ds(0, 16), jnp.where(lane3 < 32, at(0, 0), at(1, 0)))
        put(pl.ds(112, 16), jnp.where(lane3 >= 96, at(2, 7), at(1, 7)))

    def put_own(rows, value):
        field[:, rows, :] = value

    def add_left(rows, value):
        field[0:8, rows, :] = field[0:8, rows, :] + value

    def add_right(rows, value):
        field[8:16, rows, :] = field[8:16, rows, :] + value

    smooth(w_own, 0, (8, 24), put_own)

    arrive(1)
    pert_f[...] = pert_v[...].astype(F32)
    for i in range(16):
        pt[8 + i] = jnp.concatenate(columns(pert_f, i, 32), axis=0).T

    first_half = lanes_of((64, 128)) % 32 < 16

    def packed(ref, i):
        parts = [p for p in columns(ref, i, 16) for _ in range(2)]
        x = jnp.concatenate(parts, axis=0).T
        return jnp.where(first_half, x[0:64], x[64:128])

    arrive(2)
    arrive(3)
    for i in range(16):
        innov_p[i] = packed(innov_v, i)
        prec_p[i] = packed(prec_v, i)

    build(1)

    for copy in c_copies:
        copy.wait()
    p_copies = [
        remote(pt.at[pl.ds(16, 8)], pt.at[pl.ds(0, 8)], p_send.at[0], p_recv.at[0], m, right),
        remote(pt.at[pl.ds(8, 8)], pt.at[pl.ds(24, 8)], p_send.at[1], p_recv.at[1], m, left),
    ]
    for copy in p_copies:
        copy.start()
    each(0, 8, lambda i: prepare(i, xc[i]))
    each(24, 32, lambda i: prepare(i, xc[i]))
    smooth(w_left, 0, (0, 8), add_left)
    smooth(w_right, 0, (24, 32), add_right)

    for i in range(16):
        x = pt[8 + i] * field[i]
        top, bottom = x[0:64], x[64:128]
        here = jnp.where(first_half, top, bottom)
        there = jnp.where(first_half, roll(top, -16), roll(bottom, 16))
        contrib[i % 2, i // 2] = here + there

    copy = remote(contrib.at[1 - core], core_in, k_send.at[0], k_recv.at[0], sibling, t)
    copy.start()
    copy.wait()
    chip_sum[...] = contrib[core] + core_in[...]
    copies = []
    for d in range(1, 8):
        other, mem = peer(d)
        copy = remote(chip_sum.at[other], parts_in.at[chip], r_send.at[d], r_recv.at[d], mem, t)
        copy.start()
        copies.append(copy)
    for copy in copies:
        copy.wait()
    total = chip_sum[chip]
    for d in range(1, 8):
        total = total + parts_in[peer(d)[0]]

    inc_all[m] = total
    own_w[...] = prec_p[m] * (total - innov_p[m])
    a_copies = []
    for d in range(1, 8):
        other, mem = peer(d)
        copy = remote(inc_all.at[m], inc_all.at[m], a_send.at[d], a_recv.at[d], mem, t)
        copy.start()
        a_copies.append(copy)
    beside = jnp.where(chip < 4, left, right)
    slot = lax.rem(m + 8, 16)
    h_copies = []
    for d in range(8):
        other, mem = peer(d)
        copy = remote(own_w, halo_w.at[slot], h_send.at[d], h_recv.at[chip], mem, beside)
        copy.start()
        h_copies.append(copy)

    f_copies = []
    for d in range(8):
        other, mem = peer(d)
        if d:
            a_copies[d - 1].wait()
        copy = remote(inc_all.at[mem], inc_all.at[mem], f_send.at[d], f_recv.at[d], sibling, t)
        copy.start()
        f_copies.append(copy)
    g_copies = []
    for k in range(8):
        arrived = remote(own_w, halo_w.at[slot], h_send.at[k], h_recv.at[k], m, beside)
        arrived.wait_recv()
        at = lax.rem(2 * k + core + 8, 16)
        copy = remote(halo_w.at[at], halo_w.at[at], g_send.at[k], g_recv.at[k], sibling, t)
        copy.start()
        g_copies.append(copy)
    for copy in f_copies:
        copy.wait()

    def adjoint_input(i, w):
        top = jnp.where(first_half, w, roll(w, 16))
        bottom = jnp.where(first_half, roll(w, -16), w)
        prepare(i, pt[i] * jnp.concatenate([top, bottom], axis=0))

    each(0, 16, lambda i: adjoint_input(8 + i, prec_p[i] * (inc_all[i] - innov_p[i])))
    smooth(w_own, 1, (8, 24), put_own)

    for i in range(16):
        w = inc_all[i]
        top = jnp.where(first_half, w, roll(w, 16))
        bottom = jnp.where(first_half, roll(w, -16), w)
        x = jnp.concatenate([top, bottom], axis=0).T
        for q in range(4):
            inc_v[q, pl.ds(i, 16, stride=16), :] = x[32 * q : 32 * q + 16]
    stores = []

    def store(src, dst, n):
        for q in range(4):
            copy = pltpu.make_async_copy(src.at[q], dst.at[:, pl.ds(128 * q, 128)], out_sem.at[n, q])
            copy.start()
            stores.append(copy)

    store(inc_v, inc_h, 0)

    for copy in g_copies:
        copy.wait()
    for copy in h_copies:
        copy.wait_send()
    for copy in p_copies:
        copy.wait()
    each(0, 8, lambda i: adjoint_input(i, halo_w[i]))
    each(24, 32, lambda i: adjoint_input(i, halo_w[i - 16]))
    smooth(w_left, 1, (0, 8), add_left)
    smooth(w_right, 1, (24, 32), add_right)

    for i in range(16):
        x = jnp.dot(mix_t, field[i].T, precision=HIGHEST, preferred_element_type=F32)
        x = x + jnp.concatenate(columns(ctl_v, i, 32), axis=0)
        for q in range(4):
            grad_v[q, pl.ds(i, 32, stride=16), :] = x[32 * q : 32 * q + 32]
    store(grad_v, grad_h, 1)
    for copy in stores:
        copy.wait()


def local(perturbations, control, innovation, precision_field, smooth_kernel, vertical_loc):
    dma = pltpu.SemaphoreType.DMA
    anywhere = pl.BlockSpec(memory_space=pl.ANY)
    increment, gradient = pl.pallas_call(
        kernel,
        out_shape=[
            jax.ShapeDtypeStruct((256, 512), F32),
            jax.ShapeDtypeStruct((512, 512), F32),
        ],
        in_specs=[
            anywhere, anywhere, anywhere, anywhere,
            pl.BlockSpec(memory_space=pltpu.SMEM),
            pl.BlockSpec(memory_space=pltpu.VMEM),
        ],
        out_specs=[anywhere, anywhere],
        scratch_shapes=[
            pltpu.VMEM((4, 512, 128), F32),
            pltpu.VMEM((4, 512, 128), BF16),
            pltpu.VMEM((4, 512, 128), F32),
            pltpu.VMEM((4, 256, 128), F32),
            pltpu.VMEM((4, 256, 128), F32),
            pltpu.VMEM((32, 128, 128), F32),
            pltpu.VMEM((32, 128, 128), F32),
            pltpu.VMEM((32, 144, 256), BF16),
            pltpu.VMEM((2, 3, 512, 512), BF16),
            pltpu.VMEM((2, 3, 256, 256), BF16),
            pltpu.VMEM((2, 3, 256, 256), BF16),
            pltpu.VMEM((16, 128, 128), F32),
            pltpu.VMEM((2, 8, 64, 128), F32),
            pltpu.VMEM((8, 64, 128), F32),
            pltpu.VMEM((8, 64, 128), F32),
            pltpu.VMEM((8, 64, 128), F32),
            pltpu.VMEM((16, 64, 128), F32),
            pltpu.VMEM((16, 64, 128), F32),
            pltpu.VMEM((64, 128), F32),
            pltpu.VMEM((16, 64, 128), F32),
            pltpu.VMEM((16, 64, 128), F32),
            pltpu.VMEM((4, 512, 128), F32),
            pltpu.VMEM((4, 256, 128), F32),
            dma((4, 4)), dma((2, 4)),
            dma((4,)), dma((4,)),
            dma((2,)), dma((2,)),
            dma((1,)), dma((1,)),
            dma((8,)), dma((8,)),
            dma((8,)), dma((8,)),
            dma((8,)), dma((8,)),
            dma((8,)), dma((8,)),
            dma((8,)), dma((8,)),
        ],
        compiler_params=pltpu.CompilerParams(
            collective_id=0, has_side_effects=True, vmem_limit_bytes=48 * 2**20
        ),
        cost_estimate=pl.CostEstimate(flops=20 * 10**9, bytes_accessed=4 * 2**20, transcendentals=0),
        name="increment_and_gradient",
    )(
        control.reshape(512, 512),
        perturbations.reshape(512, 512),
        innovation.reshape(256, 512),
        precision_field.reshape(256, 512),
        smooth_kernel,
        vertical_loc,
    )
    return increment.reshape(16, 16, 512), gradient.reshape(2, 16, 16, 512)


def solution(mesh):
    in_specs = (
        P("mem", None, "tile", None),
        P("mem", None, "tile", None),
        P(None, "tile", None),
        P(None, "tile", None),
        P(),
        P(),
    )
    out_specs = (P(None, "tile", None), P("mem", None, "tile", None))
    return jax.shard_map(local, mesh=mesh, in_specs=in_specs, out_specs=out_specs, check_vma=False)
```

```python
import functools

import jax
import jax.numpy as jnp
from jax import lax
from jax.experimental import pallas as pl
from jax.experimental.pallas import tpu as pltpu
from jax.sharding import PartitionSpec as P

MESH = pl.DeviceIdType.MESH
HIGHEST = lax.Precision.HIGHEST
F32 = jnp.float32
BF16 = jnp.bfloat16


def lanes_of(shape):
    return lax.broadcasted_iota(jnp.int32, shape, len(shape) - 1)


def rows_of(shape):
    return lax.broadcasted_iota(jnp.int32, shape, len(shape) - 2)


def roll(x, shift):
    return pltpu.roll(x, shift % x.shape[-1], x.ndim - 1)


def composed_rows(sk, flip, variant):
    shape = (16, 1024)
    lane = lanes_of(shape)
    col = lane % 32
    start = jnp.where(lane == 264 + rows_of(shape), 1.0, 0.0).astype(F32)
    if variant == 0:
        inside = col >= 8
    elif variant == 2:
        inside = col < 24
    else:
        inside = None

    def tap(a, b):
        return sk[4 - a, 4 - b] if flip else sk[a, b]

    def one_pass(step, r):
        moved = [roll(r, 32 * (a - 2)) if a != 2 else r for a in range(5)]
        out = None
        for b in range(5):
            part = moved[0] * tap(0, b)
            for a in range(1, 5):
                part = part + moved[a] * tap(a, b)
            part = roll(part, b - 2) if b != 2 else part
            out = part if out is None else out + part
        if inside is not None:
            out = jnp.where(inside, out, 0.0)
        return out

    r = lax.fori_loop(0, 4, one_pass, start)
    total = sk[0, 0]
    for n in range(1, 25):
        total = total + sk[n // 5, n % 5]
    total = jnp.full((16, 1024), total, F32)
    square = total * total
    return r / (square * square)


def split(x):
    hi = x.astype(BF16)
    lo = (x - hi.astype(F32)).astype(BF16)
    return hi, lo


def kernel(
    ctl_h, pert_h, innov_h, prec_h, sk, vloc,
    inc_h, grad_h,
    ctl_v, pert_v, pert_f, innov_v, prec_v, pt, xb, weights, back, field,
    contrib, core_in, chip_sum, parts_in, contrib_h, core_in_h, chip_sum_h, parts_h,
    inc_all, halo_w, own_w, prec_p, innov_p, grad_v, inc_v,
    in_sem, out_sem, p_send, p_recv, k_send, k_recv, r_send, r_recv, s_send, s_recv,
    a_send, a_recv, h_send, h_recv, f_send, f_recv, g_send, g_recv,
):
    m = lax.axis_index("mem")
    t = lax.axis_index("tile")
    tiles = lax.axis_size("tile")
    right = lax.rem(t + 1, tiles)
    left = lax.rem(t + tiles - 1, tiles)
    chip = m // 2
    core = m % 2
    sibling = 2 * chip + 1 - core
    upper = chip // 4
    beside = jnp.where(chip < 4, left, right)
    opposite = jnp.where(chip < 4, right, left)

    loads = [
        [
            pltpu.make_async_copy(src.at[:, pl.ds(128 * q, 128)], dst.at[q], in_sem.at[n, q])
            for q in range(4)
        ]
        for n, (src, dst) in enumerate(
            [(pert_h, pert_v), (ctl_h, ctl_v), (innov_h, innov_v), (prec_h, prec_v)]
        )
    ]
    for load in loads:
        for copy in load:
            copy.start()

    def arrive(n):
        for copy in loads[n]:
            copy.wait()

    def peer(d):
        other = jnp.bitwise_xor(chip, d)
        return other, 2 * other + core

    barrier = pltpu.get_barrier_semaphore()

    def greet(mem, tile):
        pl.semaphore_signal(barrier, inc=1, device_id=(mem, tile), device_id_type=MESH)

    greet(sibling, t)
    for d in range(1, 8):
        greet(peer(d)[1], t)
    for k in range(8):
        greet(2 * k + core, beside)
    for k in range(4):
        greet(2 * (4 * upper + k) + core, opposite)

    pick = jnp.where(rows_of((128, 16)) % 16 == lanes_of((128, 16)), 1.0, 0.0).astype(F32)
    wide = jnp.dot(pick, vloc[...], precision=HIGHEST, preferred_element_type=F32)
    spread = jnp.where(lanes_of((16, 128)) % 16 == rows_of((16, 128)), 1.0, 0.0).astype(F32)
    full = jnp.dot(wide, spread, precision=HIGHEST, preferred_element_type=F32)
    same = rows_of((128, 128)) // 16 == lanes_of((128, 128)) // 16
    mix = jnp.where(same, full, 0.0)

    def columns(ref, i, count):
        return [ref[q, pl.ds(i, count, stride=16), :] for q in range(4)]

    def remote(src, dst, send, recv, mem, tile):
        return pltpu.make_async_remote_copy(
            src_ref=src, dst_ref=dst, send_sem=send, recv_sem=recv,
            device_id=(mem, tile), device_id_type=MESH,
        )

    def outward(ref, first, send, recv):
        to_right = first >= 16
        target = first - 16 if to_right else first + 16
        return remote(
            ref.at[pl.ds(first, 4)], ref.at[pl.ds(target, 4)], send, recv, m,
            right if to_right else left,
        )

    arrive(0)
    p_copies = []
    for n, first in enumerate((16, 12, 20, 8)):
        if n == 0:
            pert_f[...] = pert_v[...].astype(F32)
        for i in range(first, first + 4):
            pt[i] = jnp.concatenate(columns(pert_f, i - 8, 32), axis=0).T
        if n == 0:
            pl.semaphore_wait(barrier, 20)
        copy = outward(pt, first, p_send.at[n], p_recv.at[n])
        copy.start()
        p_copies.append(copy)

    lane8 = lanes_of((8, 128))

    def prepare(index, x):
        top = jnp.where(lane8 >= 32, roll(x[120:128], 32), 0.0)
        bottom = jnp.where(lane8 < 96, roll(x[0:8], -32), 0.0)
        hi, lo = split(jnp.concatenate([top, x, bottom], axis=0))
        xb[index, :, 0:128] = hi
        xb[index, :, 128:256] = lo

    def each(first, last, body):
        def step(i, carry):
            for n in range(4):
                body(4 * i + n)
            return carry

        lax.fori_loop(first // 4, last // 4, step, 0)

    arrive(1)
    for i in range(16):
        x = jnp.concatenate(columns(ctl_v, i, 32), axis=0)
        x = jnp.dot(mix, x, precision=HIGHEST, preferred_element_type=F32)
        prepare(8 + i, x.T)

    def build(direction, variant):
        base = composed_rows(sk, direction == 1, variant)
        for i in range(16):
            hi, lo = split(roll(base, 32 * i) if i else base)
            weights[direction, variant, 16 * i : 16 * i + 16, :] = hi
            weights[direction, variant, 256 + 16 * i : 272 + 16 * i, :] = lo

    for variant in range(3):
        build(0, variant)

    lane3 = lanes_of((1, 1, 128))

    def smooth(direction, spans, lons, put):
        def at(variant, b):
            w = weights.at[direction, variant]
            parts = [
                jnp.concatenate(
                    [w[at : at + 16 * (z - a), 32 * lo : 32 * hi] for lo, hi, _ in spans], axis=1
                )
                for part in range(2)
                for a, z in lons
                for at in [256 * part + 16 * a]
            ]
            lhs = jnp.concatenate(parts, axis=0)
            rhs = jnp.concatenate(
                [
                    xb[x : x + hi - lo, 16 * b : 16 * b + 32, :].reshape(32 * (hi - lo), 256)
                    for lo, hi, x in spans
                ],
                axis=0,
            )
            out = jnp.dot(lhs, rhs, preferred_element_type=F32)
            half = out.shape[0] // 2
            out = out[:half, :128] + out[:half, 128:] + out[half:, :128]
            return out.reshape(half // 16, 16, 128)

        for b in range(8):
            value = at(1, b)
            if b == 0:
                value = jnp.where(lane3 < 32, at(0, b), value)
            if b == 7:
                value = jnp.where(lane3 >= 96, at(2, b), value)
            done = 0
            for a, z in lons:
                put(a, z, 16 * b, value[done : done + z - a])
                done += z - a

    def put(a, z, row, value):
        field[8 + a : 8 + z, row : row + 16, :] = value

    def put_left(a, z, row, value):
        field[a - 8 : z - 8, row : row + 16, :] = value

    def put_right(a, z, row, value):
        field[24 + a : 24 + z, row : row + 16, :] = value

    def add(a, z, row, value):
        field[8 + a : 8 + z, row : row + 16, :] = field[8 + a : 8 + z, row : row + 16, :] + value

    every = [(0, 16)]
    outer = [(0, 4), (12, 16)]
    smooth(0, [(8, 24, 8)], every, put)
    smooth(0, [(24, 32, 8)], [(8, 16)], put_left)
    smooth(0, [(0, 8, 16)], [(0, 8)], put_right)

    first_half = lanes_of((64, 128)) % 32 < 16
    inner_first = [[4 + k for k in range(8)], [k if k < 4 else k + 8 for k in range(8)]]

    halo_first = [
        [28 + k if k < 4 else k - 4 for k in range(8)],
        [24 + k if k < 4 else k for k in range(8)],
    ]

    def members(i):
        x = pt[i] * field[i]
        top, bottom = x[0:64], x[64:128]
        here = jnp.where(first_half, top, bottom)
        there = jnp.where(first_half, roll(top, -16), roll(bottom, 16))
        return here + there

    def to_sibling(src, dst, n):
        copy = remote(src.at[1 - core], dst, k_send.at[n], k_recv.at[n], sibling, t)
        copy.start()
        return copy

    def contribute_halo(g):
        for k, i in enumerate(halo_first[g]):
            both = members(i)
            contrib_h[g, 0, k] = both[0:32]
            contrib_h[g, 1, k] = both[32:64]
        return to_sibling(contrib_h.at[g], core_in_h.at[g], g)

    def scatter_halo(g, copy):
        copy.wait()
        chip_sum_h[g] = contrib_h[g, core] + core_in_h[g]
        copies = []
        for k in range(8):
            copy = remote(
                chip_sum_h.at[g, k], parts_h.at[g, chip], s_send.at[g, k], s_recv.at[g, chip],
                2 * k + core, right if k < 4 else left,
            )
            copy.start()
            copies.append(copy)
        return copies

    def spread_total(g, copies):
        for copy in copies:
            copy.wait_send()
        total = chip_sum[chip, g]
        for d in range(1, 8):
            total = total + parts_in[peer(d)[0], g]
        for k in range(8):
            remote(
                chip_sum_h.at[g, k], parts_h.at[g, k], s_send.at[g, k], s_recv.at[g, k], m, beside
            ).wait_recv()
        for k in range(8):
            total = total + parts_h[g, k]
        inc_all[g, chip, core] = total
        lon = 4 + chip if g == 0 else chip + 8 * (chip // 4)
        own_w[g] = prec_p[lon, core] * (total - innov_p[lon, core])
        a_copies = []
        for d in range(1, 8):
            mem = peer(d)[1]
            piece = inc_all.at[g, chip, core]
            copy = remote(piece, piece, a_send.at[g, d], a_recv.at[g, d], mem, t)
            copy.start()
            a_copies.append(copy)
        h_copies = []
        for d in range(8):
            copy = remote(
                own_w.at[g], halo_w.at[g, chip, core],
                h_send.at[g, d], h_recv.at[g, chip], peer(d)[1], beside,
            )
            copy.start()
            h_copies.append(copy)
        return a_copies, h_copies

    def pass_total(g, a_copies):
        for copy in a_copies:
            copy.wait()
        piece = inc_all.at[g, pl.ds(0, 8), core]
        copy = remote(piece, piece, f_send.at[g], f_recv.at[g], sibling, t)
        copy.start()
        return copy

    def pass_halo(g, h_copies):
        for copy in h_copies:
            copy.wait_send()
        for k in range(8):
            remote(
                own_w.at[g], halo_w.at[g, chip, core],
                h_send.at[g, k], h_recv.at[g, k], m, beside,
            ).wait_recv()
        piece = halo_w.at[g, pl.ds(0, 8), core]
        copy = remote(piece, piece, g_send.at[g], g_recv.at[g], sibling, t)
        copy.start()
        return copy

    for g in range(2):
        for k, i in enumerate(inner_first[g]):
            both = members(8 + i)
            contrib[0, k, g] = both[0:32]
            contrib[1, k, g] = both[32:64]
    k_copy = to_sibling(contrib, core_in, 2)

    def pack(ref, out, i):
        parts = [p for p in columns(ref, i, 16) for _ in range(2)]
        x = jnp.concatenate(parts, axis=0).T
        x = jnp.where(first_half, x[0:64], x[64:128])
        out[i, 0] = x[0:32]
        out[i, 1] = x[32:64]

    arrive(2)
    arrive(3)
    for i in range(8):
        pack(innov_v, innov_p, i)
        pack(prec_v, prec_p, i)

    k_copy.wait()
    chip_sum[...] = contrib[core] + core_in[...]
    r_copies = []
    for d in range(1, 8):
        other, mem = peer(d)
        copy = remote(
            chip_sum.at[other], parts_in.at[chip], r_send.at[d], r_recv.at[d], mem, t
        )
        copy.start()
        r_copies.append(copy)

    for copy in p_copies[:2]:
        copy.wait()
    k_copy_0 = contribute_halo(0)
    for i in range(8, 16):
        pack(innov_v, innov_p, i)
        pack(prec_v, prec_p, i)
    s_copies_0 = scatter_halo(0, k_copy_0)
    for copy in p_copies[2:]:
        copy.wait()
    k_copy_1 = contribute_halo(1)
    s_copies_1 = scatter_halo(1, k_copy_1)

    build(1, 1)
    for copy in r_copies:
        copy.wait()
    a_copies_0, h_copies_0 = spread_total(0, s_copies_0)
    build(1, 0)
    build(1, 2)
    a_copies_1, h_copies_1 = spread_total(1, s_copies_1)
    f_copy_0 = pass_total(0, a_copies_0)
    g_copy_0 = pass_halo(0, h_copies_0)

    def unpack(w):
        top = jnp.where(first_half, w, roll(w, 16))
        bottom = jnp.where(first_half, roll(w, -16), w)
        return jnp.concatenate([top, bottom], axis=0)

    def own_input(g, k, lon):
        total = inc_all[g, k].reshape(64, 128)
        w = prec_p[lon].reshape(64, 128) * (total - innov_p[lon].reshape(64, 128))
        prepare(8 + lon, pt[8 + lon] * unpack(w))

    def halo_input(g, k, index):
        prepare(index, pt[index] * unpack(halo_w[g, k].reshape(64, 128)))

    def show(g):
        for k, i in enumerate(inner_first[g]):
            x = unpack(inc_all[g, k].reshape(64, 128)).T
            for q in range(4):
                inc_v[q, pl.ds(i, 16, stride=16), :] = x[32 * q : 32 * q + 16]

    f_copy_0.wait()
    each(0, 8, lambda k: own_input(0, k, k + 4))
    smooth(1, [(12, 20, 12)], every, put)
    g_copy_0.wait()
    each(0, 4, lambda k: halo_input(0, k, 28 + k))
    each(4, 8, lambda k: halo_input(0, k, k - 4))
    smooth(1, [(0, 4, 0), (28, 32, 28)], outer, add)
    show(0)

    f_copy_1 = pass_total(1, a_copies_1)
    g_copy_1 = pass_halo(1, h_copies_1)
    f_copy_1.wait()
    each(0, 4, lambda k: own_input(1, k, k))
    each(4, 8, lambda k: own_input(1, k, k + 8))
    g_copy_1.wait()
    each(0, 4, lambda k: halo_input(1, k, 24 + k))
    each(4, 8, lambda k: halo_input(1, k, k))
    smooth(1, [(4, 12, 4), (20, 28, 20)], every, add)

    show(1)
    stores = []

    def store(src, dst, n):
        for q in range(4):
            copy = pltpu.make_async_copy(src.at[q], dst.at[:, pl.ds(128 * q, 128)], out_sem.at[n, q])
            copy.start()
            stores.append(copy)

    store(inc_v, inc_h, 0)

    hi, lo = split(mix.T)
    back[0:128, 0:128] = hi
    back[0:128, 128:256] = hi
    back[128:256, 0:128] = lo
    back[128:256, 128:256] = jnp.zeros((128, 128), BF16)
    for i in range(0, 16, 2):
        hi, lo = split(field[8 + i : 10 + i].reshape(256, 128))
        x = lax.dot_general(
            back[...], jnp.concatenate([hi, lo], axis=1), (((1,), (1,)), ((), ())),
            preferred_element_type=F32,
        )
        x = x[0:128] + x[128:256]
        for n in range(2):
            old = columns(ctl_v, i + n, 32)
            for q in range(4):
                grad_v[q, pl.ds(i + n, 32, stride=16), :] = (
                    x[32 * q : 32 * q + 32, 128 * n : 128 * n + 128] + old[q]
                )
    store(grad_v, grad_h, 1)
    for copy in stores:
        copy.wait()


def local(perturbations, control, innovation, precision_field, smooth_kernel, vertical_loc):
    dma = pltpu.SemaphoreType.DMA
    anywhere = pl.BlockSpec(memory_space=pltpu.HBM)
    increment, gradient = pl.pallas_call(
        kernel,
        out_shape=[
            jax.ShapeDtypeStruct((256, 512), F32),
            jax.ShapeDtypeStruct((512, 512), F32),
        ],
        in_specs=[
            anywhere, anywhere, anywhere, anywhere,
            pl.BlockSpec(memory_space=pltpu.SMEM),
            pl.BlockSpec(memory_space=pltpu.VMEM),
        ],
        out_specs=[anywhere, anywhere],
        scratch_shapes=[
            pltpu.VMEM((4, 512, 128), F32),
            pltpu.VMEM((4, 512, 128), BF16),
            pltpu.VMEM((4, 512, 128), F32),
            pltpu.VMEM((4, 256, 128), F32),
            pltpu.VMEM((4, 256, 128), F32),
            pltpu.VMEM((32, 128, 128), F32),
            pltpu.VMEM((32, 144, 256), BF16),
            pltpu.VMEM((2, 3, 512, 1024), BF16),
            pltpu.VMEM((256, 256), BF16),
            pltpu.VMEM((32, 128, 128), F32),
            pltpu.VMEM((2, 8, 2, 32, 128), F32),
            pltpu.VMEM((8, 2, 32, 128), F32),
            pltpu.VMEM((8, 2, 32, 128), F32),
            pltpu.VMEM((8, 2, 32, 128), F32),
            pltpu.VMEM((2, 2, 8, 32, 128), F32),
            pltpu.VMEM((2, 8, 32, 128), F32),
            pltpu.VMEM((2, 8, 32, 128), F32),
            pltpu.VMEM((2, 8, 32, 128), F32),
            pltpu.VMEM((2, 8, 2, 32, 128), F32),
            pltpu.VMEM((2, 8, 2, 32, 128), F32),
            pltpu.VMEM((2, 32, 128), F32),
            pltpu.VMEM((16, 2, 32, 128), F32),
            pltpu.VMEM((16, 2, 32, 128), F32),
            pltpu.VMEM((4, 512, 128), F32),
            pltpu.VMEM((4, 256, 128), F32),
            dma((4, 4)), dma((2, 4)),
            dma((4,)), dma((4,)),
            dma((3,)), dma((3,)),
            dma((8,)), dma((8,)),
            dma((2, 8)), dma((2, 8)),
            dma((2, 8)), dma((2, 8)),
            dma((2, 8)), dma((2, 8)),
            dma((2,)), dma((2,)),
            dma((2,)), dma((2,)),
        ],
        compiler_params=pltpu.CompilerParams(
            collective_id=0, has_side_effects=True, vmem_limit_bytes=64 * 2**20
        ),
        cost_estimate=pl.CostEstimate(flops=20 * 10**9, bytes_accessed=4 * 2**20, transcendentals=0),
        name="increment_and_gradient",
    )(
        control.reshape(512, 512),
        perturbations.reshape(512, 512),
        innovation.reshape(256, 512),
        precision_field.reshape(256, 512),
        smooth_kernel,
        vertical_loc,
    )
    return increment.reshape(16, 16, 512), gradient.reshape(2, 16, 16, 512)


def solution(mesh):
    in_specs = (
        P("mem", None, "tile", None),
        P("mem", None, "tile", None),
        P(None, "tile", None),
        P(None, "tile", None),
        P(),
        P(),
    )
    out_specs = (P(None, "tile", None), P("mem", None, "tile", None))
    return jax.shard_map(local, mesh=mesh, in_specs=in_specs, out_specs=out_specs, check_vma=False)
```

```python
import functools

import jax
import jax.numpy as jnp
from jax import lax
from jax.experimental import pallas as pl
from jax.experimental.pallas import tpu as pltpu
from jax.sharding import PartitionSpec as P

MESH = pl.DeviceIdType.MESH
HIGHEST = lax.Precision.HIGHEST
F32 = jnp.float32
BF16 = jnp.bfloat16


def lanes_of(shape):
    return lax.broadcasted_iota(jnp.int32, shape, len(shape) - 1)


def rows_of(shape):
    return lax.broadcasted_iota(jnp.int32, shape, len(shape) - 2)


def roll(x, shift):
    return pltpu.roll(x, shift % x.shape[-1], x.ndim - 1)


def composed_rows(sk, flip):
    shape = (24, 640)
    lane = lanes_of(shape)
    band = rows_of(shape) // 8
    j = rows_of(shape) % 8 + jnp.where(band == 2, 8, 0)
    col = lane % 32
    start = jnp.where(lane == 264 + j, 1.0, 0.0).astype(F32)
    outside = ((band == 0) & (col < 8)) | ((band == 2) & (col >= 24))

    def tap(a, b):
        return sk[4 - a, 4 - b] if flip else sk[a, b]

    def one_pass(step, r):
        moved = [roll(r, 32 * (a - 2)) if a != 2 else r for a in range(5)]
        out = None
        for b in range(5):
            part = moved[0] * tap(0, b)
            for a in range(1, 5):
                part = part + moved[a] * tap(a, b)
            part = roll(part, b - 2) if b != 2 else part
            out = part if out is None else out + part
        return jnp.where(outside, 0.0, out)

    r = lax.fori_loop(0, 4, one_pass, start)
    total = sk[0, 0]
    for n in range(1, 25):
        total = total + sk[n // 5, n % 5]
    total = jnp.full(shape, total, F32)
    square = total * total
    return r / (square * square)


def split(x):
    hi = x.astype(BF16)
    lo = (x - hi.astype(F32)).astype(BF16)
    return hi, lo


def kernel(
    ctl_h, pert_h, innov_h, prec_h, sk, vloc,
    inc_v, grad_v,
    ctl_v, pert_v, pert_f, innov_v, prec_v, pt, xb, weights, back, field,
    contrib, core_in, chip_sum, parts_in, contrib_h, core_in_h, chip_sum_h, parts_h,
    inc_all, halo_w, own_w, prec_p, innov_p,
    in_sem, p_send, p_recv, k_send, k_recv, r_send, r_recv, s_send, s_recv,
    a_send, a_recv, h_send, h_recv, f_send, f_recv, g_send, g_recv,
):
    m = lax.axis_index("mem")
    t = lax.axis_index("tile")
    tiles = lax.axis_size("tile")
    right = lax.rem(t + 1, tiles)
    left = lax.rem(t + tiles - 1, tiles)
    chip = m // 2
    core = m % 2
    sibling = 2 * chip + 1 - core
    upper = chip // 4
    beside = jnp.where(chip < 4, left, right)
    opposite = jnp.where(chip < 4, right, left)

    loads = [
        [
            pltpu.make_async_copy(src.at[:, pl.ds(128 * q, 128)], dst.at[q], in_sem.at[n, q])
            for q in range(4)
        ]
        for n, (src, dst) in enumerate(
            [(pert_h, pert_v), (ctl_h, ctl_v), (innov_h, innov_v), (prec_h, prec_v)]
        )
    ]
    for load in loads:
        for copy in load:
            copy.start()

    def arrive(n):
        for copy in loads[n]:
            copy.wait()

    def peer(d):
        other = jnp.bitwise_xor(chip, d)
        return other, 2 * other + core

    barrier = pltpu.get_barrier_semaphore()

    def greet(mem, tile):
        pl.semaphore_signal(barrier, inc=1, device_id=(mem, tile), device_id_type=MESH)

    greet(sibling, t)
    for d in range(1, 8):
        greet(peer(d)[1], t)
    for k in range(8):
        greet(2 * k + core, beside)
    for k in range(4):
        greet(2 * (4 * upper + k) + core, opposite)

    pick = jnp.where(rows_of((128, 16)) % 16 == lanes_of((128, 16)), 1.0, 0.0).astype(F32)
    wide = jnp.dot(pick, vloc[...], precision=HIGHEST, preferred_element_type=F32)
    spread = jnp.where(lanes_of((16, 128)) % 16 == rows_of((16, 128)), 1.0, 0.0).astype(F32)
    full = jnp.dot(wide, spread, precision=HIGHEST, preferred_element_type=F32)
    same = rows_of((128, 128)) // 16 == lanes_of((128, 128)) // 16
    mix = jnp.where(same, full, 0.0)

    def columns(ref, i, count):
        return [ref[q, pl.ds(i, count, stride=16), :] for q in range(4)]

    def remote(src, dst, send, recv, mem, tile):
        return pltpu.make_async_remote_copy(
            src_ref=src, dst_ref=dst, send_sem=send, recv_sem=recv,
            device_id=(mem, tile), device_id_type=MESH,
        )

    def outward(ref, first, send, recv):
        to_right = first >= 16
        target = first - 16 if to_right else first + 16
        return remote(
            ref.at[pl.ds(first, 4)], ref.at[pl.ds(target, 4)], send, recv, m,
            right if to_right else left,
        )

    arrive(0)
    p_copies = []
    for n, first in enumerate((16, 12, 20, 8)):
        if n == 0:
            pert_f[...] = pert_v[...].astype(F32)
        for i in range(first, first + 4):
            pt[i] = jnp.concatenate(columns(pert_f, i - 8, 32), axis=0).T
        if n == 0:
            pl.semaphore_wait(barrier, 20)
        copy = outward(pt, first, p_send.at[n], p_recv.at[n])
        copy.start()
        p_copies.append(copy)

    lane8 = lanes_of((8, 128))

    def prepare(index, x):
        top = jnp.where(lane8 >= 32, roll(x[120:128], 32), 0.0)
        bottom = jnp.where(lane8 < 96, roll(x[0:8], -32), 0.0)
        hi, lo = split(jnp.concatenate([top, x, bottom], axis=0))
        xb[index, :, 0:128] = hi
        xb[index, :, 128:256] = lo

    def each(first, last, body):
        def step(i, carry):
            for n in range(4):
                body(4 * i + n)
            return carry

        lax.fori_loop(first // 4, last // 4, step, 0)

    arrive(1)
    for i in range(16):
        x = jnp.concatenate(columns(ctl_v, i, 32), axis=0)
        x = jnp.dot(mix, x, precision=HIGHEST, preferred_element_type=F32)
        prepare(8 + i, x.T)

    def build(direction):
        rows = composed_rows(sk, direction == 1)
        first, inside, last = rows[0:8], rows[8:16], rows[16:24]
        shifted = roll(inside, 8)
        for variant, halves in enumerate([(first, shifted), (inside, shifted), (inside, last)]):
            base = jnp.concatenate(halves, axis=0)
            for n in range(4):
                for part, value in enumerate(split(roll(base, 32 * n) if n else base)):
                    for i in range(n, 16, 4):
                        at = 256 * part + 16 * i
                        lane = 32 * (i - n)
                        if lane:
                            weights[direction, variant, at : at + 16, 0:lane] = jnp.zeros((16, lane), BF16)
                        weights[direction, variant, at : at + 16, lane : lane + 640] = value
                        rest = 1024 - lane - 640
                        if rest:
                            weights[direction, variant, at : at + 16, lane + 640 : 1024] = jnp.zeros(
                                (16, rest), BF16
                            )

    build(0)

    lane3 = lanes_of((1, 1, 128))

    def smooth(direction, spans, lons, put):
        def at(variant, b):
            w = weights.at[direction, variant]
            parts = [
                jnp.concatenate(
                    [w[at : at + 16 * (z - a), 32 * lo : 32 * hi] for lo, hi, _ in spans], axis=1
                )
                for part in range(2)
                for a, z in lons
                for at in [256 * part + 16 * a]
            ]
            lhs = jnp.concatenate(parts, axis=0)
            rhs = jnp.concatenate(
                [
                    xb[x : x + hi - lo, 16 * b : 16 * b + 32, :].reshape(32 * (hi - lo), 256)
                    for lo, hi, x in spans
                ],
                axis=0,
            )
            out = jnp.dot(lhs, rhs, preferred_element_type=F32)
            half = out.shape[0] // 2
            out = out[:half, :128] + out[:half, 128:] + out[half:, :128]
            return out.reshape(half // 16, 16, 128)

        for b in range(8):
            value = at(1, b)
            if b == 0:
                value = jnp.where(lane3 < 32, at(0, b), value)
            if b == 7:
                value = jnp.where(lane3 >= 96, at(2, b), value)
            done = 0
            for a, z in lons:
                put(a, z, 16 * b, value[done : done + z - a])
                done += z - a

    def put(a, z, row, value):
        field[8 + a : 8 + z, row : row + 16, :] = value

    def put_left(a, z, row, value):
        field[a - 8 : z - 8, row : row + 16, :] = value

    def put_right(a, z, row, value):
        field[24 + a : 24 + z, row : row + 16, :] = value

    def add(a, z, row, value):
        field[8 + a : 8 + z, row : row + 16, :] = field[8 + a : 8 + z, row : row + 16, :] + value

    every = [(0, 16)]
    outer = [(0, 4), (12, 16)]
    smooth(0, [(8, 24, 8)], every, put)
    smooth(0, [(24, 32, 8)], [(8, 16)], put_left)
    smooth(0, [(0, 8, 16)], [(0, 8)], put_right)

    first_half = lanes_of((64, 128)) % 32 < 16
    inner_first = [[4 + k for k in range(8)], [k if k < 4 else k + 8 for k in range(8)]]

    halo_first = [
        [28 + k if k < 4 else k - 4 for k in range(8)],
        [24 + k if k < 4 else k for k in range(8)],
    ]

    def members(i):
        x = pt[i] * field[i]
        top, bottom = x[0:64], x[64:128]
        here = jnp.where(first_half, top, bottom)
        there = jnp.where(first_half, roll(top, -16), roll(bottom, 16))
        return here + there

    def to_sibling(src, dst, n):
        copy = remote(src.at[1 - core], dst, k_send.at[n], k_recv.at[n], sibling, t)
        copy.start()
        return copy

    def contribute_halo(g):
        for k, i in enumerate(halo_first[g]):
            both = members(i)
            contrib_h[g, 0, k] = both[0:32]
            contrib_h[g, 1, k] = both[32:64]
        return to_sibling(contrib_h.at[g], core_in_h.at[g], g)

    def scatter_halo(g, copy):
        copy.wait()
        chip_sum_h[g] = contrib_h[g, core] + core_in_h[g]
        copies = []
        for k in range(8):
            copy = remote(
                chip_sum_h.at[g, k], parts_h.at[g, chip], s_send.at[g, k], s_recv.at[g, chip],
                2 * k + core, right if k < 4 else left,
            )
            copy.start()
            copies.append(copy)
        return copies

    def spread_total(g, copies):
        for copy in copies:
            copy.wait_send()
        total = chip_sum[chip, g]
        for d in range(1, 8):
            total = total + parts_in[peer(d)[0], g]
        for k in range(8):
            remote(
                chip_sum_h.at[g, k], parts_h.at[g, k], s_send.at[g, k], s_recv.at[g, k], m, beside
            ).wait_recv()
        for k in range(8):
            total = total + parts_h[g, k]
        inc_all[g, chip, core] = total
        lon = 4 + chip if g == 0 else chip + 8 * (chip // 4)
        own_w[g] = prec_p[lon, core] * (total - innov_p[lon, core])
        h_copies = []
        for d in range(8):
            copy = remote(
                own_w.at[g], halo_w.at[g, chip, core],
                h_send.at[g, d], h_recv.at[g, chip], peer(d)[1], beside,
            )
            copy.start()
            h_copies.append(copy)
        a_copies = []
        for d in range(1, 8):
            mem = peer(d)[1]
            piece = inc_all.at[g, chip, core]
            copy = remote(piece, piece, a_send.at[g, d], a_recv.at[g, d], mem, t)
            copy.start()
            a_copies.append(copy)
        return a_copies, h_copies

    def pass_total(g, a_copies):
        for copy in a_copies:
            copy.wait()
        piece = inc_all.at[g, pl.ds(0, 8), core]
        copy = remote(piece, piece, f_send.at[g], f_recv.at[g], sibling, t)
        copy.start()
        return copy

    def pass_halo(g, h_copies):
        for copy in h_copies:
            copy.wait_send()
        for k in range(8):
            remote(
                own_w.at[g], halo_w.at[g, chip, core],
                h_send.at[g, k], h_recv.at[g, k], m, beside,
            ).wait_recv()
        piece = halo_w.at[g, pl.ds(0, 8), core]
        copy = remote(piece, piece, g_send.at[g], g_recv.at[g], sibling, t)
        copy.start()
        return copy

    for g in range(2):
        for k, i in enumerate(inner_first[g]):
            both = members(8 + i)
            contrib[0, k, g] = both[0:32]
            contrib[1, k, g] = both[32:64]
    k_copy = to_sibling(contrib, core_in, 2)

    def pack(ref, out, i):
        parts = [p for p in columns(ref, i, 16) for _ in range(2)]
        x = jnp.concatenate(parts, axis=0).T
        x = jnp.where(first_half, x[0:64], x[64:128])
        out[i, 0] = x[0:32]
        out[i, 1] = x[32:64]

    arrive(2)
    arrive(3)
    for i in range(4):
        pack(innov_v, innov_p, i)
        pack(prec_v, prec_p, i)

    k_copy.wait()
    chip_sum[...] = contrib[core] + core_in[...]
    r_copies = []
    for d in range(1, 8):
        other, mem = peer(d)
        copy = remote(
            chip_sum.at[other], parts_in.at[chip], r_send.at[d], r_recv.at[d], mem, t
        )
        copy.start()
        r_copies.append(copy)

    for copy in p_copies[:2]:
        copy.wait()
    k_copy_0 = contribute_halo(0)
    for i in range(4, 10):
        pack(innov_v, innov_p, i)
        pack(prec_v, prec_p, i)
    s_copies_0 = scatter_halo(0, k_copy_0)
    for i in range(10, 16):
        pack(innov_v, innov_p, i)
        pack(prec_v, prec_p, i)
    for copy in p_copies[2:]:
        copy.wait()
    k_copy_1 = contribute_halo(1)
    build(1)
    s_copies_1 = scatter_halo(1, k_copy_1)

    hi, lo = split(mix.T)
    back[0:128, 0:128] = hi
    back[0:128, 128:256] = hi
    back[128:256, 0:128] = lo
    back[128:256, 128:256] = jnp.zeros((128, 128), BF16)

    for copy in r_copies:
        copy.wait()
    a_copies_0, h_copies_0 = spread_total(0, s_copies_0)
    a_copies_1, h_copies_1 = spread_total(1, s_copies_1)
    f_copy_0 = pass_total(0, a_copies_0)
    g_copy_0 = pass_halo(0, h_copies_0)

    def unpack(w):
        top = jnp.where(first_half, w, roll(w, 16))
        bottom = jnp.where(first_half, roll(w, -16), w)
        return jnp.concatenate([top, bottom], axis=0)

    def own_input(g, k, lon):
        total = inc_all[g, k].reshape(64, 128)
        w = prec_p[lon].reshape(64, 128) * (total - innov_p[lon].reshape(64, 128))
        prepare(8 + lon, pt[8 + lon] * unpack(w))

    def halo_input(g, k, index):
        prepare(index, pt[index] * unpack(halo_w[g, k].reshape(64, 128)))

    def show(g):
        for k, i in enumerate(inner_first[g]):
            x = unpack(inc_all[g, k].reshape(64, 128)).T
            for q in range(4):
                inc_v[q, pl.ds(i, 16, stride=16), :] = x[32 * q : 32 * q + 16]

    f_copy_0.wait()
    each(0, 8, lambda k: own_input(0, k, k + 4))
    smooth(1, [(12, 20, 12)], every, put)
    g_copy_0.wait()
    each(0, 4, lambda k: halo_input(0, k, 28 + k))
    each(4, 8, lambda k: halo_input(0, k, k - 4))
    smooth(1, [(0, 4, 0), (28, 32, 28)], outer, add)
    show(0)

    f_copy_1 = pass_total(1, a_copies_1)
    g_copy_1 = pass_halo(1, h_copies_1)
    f_copy_1.wait()
    each(0, 4, lambda k: own_input(1, k, k))
    each(4, 8, lambda k: own_input(1, k, k + 8))
    smooth(1, [(8, 12, 8), (20, 24, 20)], every, add)
    g_copy_1.wait()
    each(0, 4, lambda k: halo_input(1, k, 24 + k))
    each(4, 8, lambda k: halo_input(1, k, k))
    smooth(1, [(4, 8, 4), (24, 28, 24)], every, add)

    show(1)
    for i in range(0, 16, 2):
        hi, lo = split(field[8 + i : 10 + i].reshape(256, 128))
        x = lax.dot_general(
            back[...], jnp.concatenate([hi, lo], axis=1), (((1,), (1,)), ((), ())),
            preferred_element_type=F32,
        )
        x = x[0:128] + x[128:256]
        for n in range(2):
            old = columns(ctl_v, i + n, 32)
            for q in range(4):
                grad_v[q, pl.ds(i + n, 32, stride=16), :] = (
                    x[32 * q : 32 * q + 32, 128 * n : 128 * n + 128] + old[q]
                )


def local(perturbations, control, innovation, precision_field, smooth_kernel, vertical_loc):
    dma = pltpu.SemaphoreType.DMA
    anywhere = pl.BlockSpec(memory_space=pltpu.HBM)
    increment, gradient = pl.pallas_call(
        kernel,
        out_shape=[
            pltpu.VMEM((4, 256, 128), F32),
            pltpu.VMEM((4, 512, 128), F32),
        ],
        in_specs=[
            anywhere, anywhere, anywhere, anywhere,
            pl.BlockSpec(memory_space=pltpu.SMEM),
            pl.BlockSpec(memory_space=pltpu.VMEM),
        ],
        out_specs=[pl.BlockSpec(memory_space=pltpu.VMEM)] * 2,
        scratch_shapes=[
            pltpu.VMEM((4, 512, 128), F32),
            pltpu.VMEM((4, 512, 128), BF16),
            pltpu.VMEM((4, 512, 128), F32),
            pltpu.VMEM((4, 256, 128), F32),
            pltpu.VMEM((4, 256, 128), F32),
            pltpu.VMEM((32, 128, 128), F32),
            pltpu.VMEM((32, 144, 256), BF16),
            pltpu.VMEM((2, 3, 512, 1024), BF16),
            pltpu.VMEM((256, 256), BF16),
            pltpu.VMEM((32, 128, 128), F32),
            pltpu.VMEM((2, 8, 2, 32, 128), F32),
            pltpu.VMEM((8, 2, 32, 128), F32),
            pltpu.VMEM((8, 2, 32, 128), F32),
            pltpu.VMEM((8, 2, 32, 128), F32),
            pltpu.VMEM((2, 2, 8, 32, 128), F32),
            pltpu.VMEM((2, 8, 32, 128), F32),
            pltpu.VMEM((2, 8, 32, 128), F32),
            pltpu.VMEM((2, 8, 32, 128), F32),
            pltpu.VMEM((2, 8, 2, 32, 128), F32),
            pltpu.VMEM((2, 8, 2, 32, 128), F32),
            pltpu.VMEM((2, 32, 128), F32),
            pltpu.VMEM((16, 2, 32, 128), F32),
            pltpu.VMEM((16, 2, 32, 128), F32),
            dma((4, 4)),
            dma((4,)), dma((4,)),
            dma((3,)), dma((3,)),
            dma((8,)), dma((8,)),
            dma((2, 8)), dma((2, 8)),
            dma((2, 8)), dma((2, 8)),
            dma((2, 8)), dma((2, 8)),
            dma((2,)), dma((2,)),
            dma((2,)), dma((2,)),
        ],
        compiler_params=pltpu.CompilerParams(
            collective_id=0, has_side_effects=True, vmem_limit_bytes=58 * 2**20
        ),
        cost_estimate=pl.CostEstimate(flops=20 * 10**9, bytes_accessed=4 * 2**20, transcendentals=0),
        name="increment_and_gradient",
    )(
        control.reshape(512, 512),
        perturbations.reshape(512, 512),
        innovation.reshape(256, 512),
        precision_field.reshape(256, 512),
        smooth_kernel,
        vertical_loc,
    )
    increment = jnp.concatenate([increment[q] for q in range(4)], axis=1)
    gradient = jnp.concatenate([gradient[q] for q in range(4)], axis=1)
    return increment.reshape(16, 16, 512), gradient.reshape(2, 16, 16, 512)


def solution(mesh):
    in_specs = (
        P("mem", None, "tile", None),
        P("mem", None, "tile", None),
        P(None, "tile", None),
        P(None, "tile", None),
        P(),
        P(),
    )
    out_specs = (P(None, "tile", None), P("mem", None, "tile", None))
    return jax.shard_map(local, mesh=mesh, in_specs=in_specs, out_specs=out_specs, check_vma=False)
```
